32 devices in a mesh: lat: 4 (over z), lon: 4 (over x, core), ens: 2 (over y).
Axes of the slice: x: 2, y: 2, z: 4, core: 2. Of those that a mesh axis runs over, the one named last changes fastest.
Arguments:
- initial_state: bfloat16 [2, 128, 256, 256], P('ens', 'lat', 'lon'), may hold values from -6 to 6
- background: bfloat16 [2, 128, 256, 256], P('ens', 'lat', 'lon'), may hold values from -6 to 6
- background_precision: float32 [256], replicated, may hold values from 0.5 to 4
- kernel_taps: float32 [2, 25, 256], replicated, may hold values from -1 to 1
- norm_gains: float32 [2, 256], replicated, may hold values from 0.5 to 2
- weight_in: bfloat16 [2, 256, 512], replicated, may hold values from -0.375 to 0.375
- weight_out: bfloat16 [2, 512, 256], replicated, may hold values from -0.25 to 0.25
- obs_operator: bfloat16 [256, 128], replicated, may hold values from -0.375 to 0.375
- obs_precision: float32 [128], replicated, may hold values from 0.5 to 4
- obs_values: bfloat16 [8192, 128], P(('lat', 'lon')), may hold values from -6 to 6
- obs_owner: int32 [8192, 1], P(('lat', 'lon')), may hold values from 0 to 15; in each aligned block of 512 rows (0 to 511, 512 to 1023, ...) at most 64 rows name the same one
- obs_cell: int32 [8192], P(('lat', 'lon')), may hold values from 0 to 2047
Outputs:
- gradient: float32 [2, 128, 256, 256], P('ens', 'lat', 'lon')
The draws below stay inside these ranges and needn't reach their ends.
Inputs may be any that keep to these rules, and one draw needn't show every extreme that they name: `obs_owner`: among the 512 footprints of one device, no owner is named more than 64 times; in every draw some device names one owner exactly 64 times. Owner numbers run over the lat index times the lon axis's device count plus the lon index. `obs_cell`: cells are numbered row by row over the owner's 32 x 64 block.
All inputs are finite; a program needn't handle non-finite values.
Results may differ from the reference program's by a relative error of at most 0.006.
Values may be sent and summed in bfloat16 or wider, within the bound.
A program may use at most 128 MiB of HBM per device.

```python
import math
import jax
import jax.numpy as jnp
import numpy as np
from jax import lax

C = 256
HID = 512
K = 128
KERNEL = 25
LAYERS = 2
CLAT = 32
OBS_DEV = 512
CLON = 64
NLAT = 128
NLON = 256
ENS = 2
NGRID = 16
CAP = 64
OBS = 8192
N_LON = 4


def place_ends(values, key, low, top_value):
    longest = values.shape.index(max(values.shape))
    spots = []
    for shift in (0, 1):
        where = [jax.random.randint(jax.random.fold_in(key, axis), (), 0, length) for axis, length in enumerate(values.shape)]
        where[longest] = (where[longest] + shift) % values.shape[longest]
        spots.append(tuple(where))
    return values.at[spots[0]].set(low).at[spots[1]].set(top_value)


def block_levels(own_key, extent, pieces, least, high):
    level, own = 1.0, jax.random.fold_in(own_key, 6)
    for axis_at, parts in pieces:
        heights = jnp.exp(jax.random.uniform(jax.random.fold_in(own, axis_at), (parts,), jnp.float32, least / len(pieces), high / len(pieces)))
        level = level * jnp.repeat(heights, extent[axis_at] // parts).reshape([-1 if axis == axis_at else 1 for axis in range(len(extent))])
    return level


def assign_block(rng, own, number, rows, number_of, top, bound, lean):
    sequence = jax.random.permutation(rng, number_of)
    crowded, usual = load_shares(number_of, rows * top, bound, lean, True), load_shares(number_of, rows * top, bound, lean, False)
    places = jnp.arange(number_of)

    def named(lengths, rotation):
        used = int((lengths > 0).sum())
        fixed = max(1, used // 4)
        shifted = fixed + (places - fixed + rotation * (used - fixed)) % max(1, number_of - fixed)
        return jnp.zeros((number_of,), jnp.int32).at[sequence[jnp.where(places < fixed, places, shifted)]].set(jnp.asarray(lengths, jnp.int32))

    lengths = jnp.where(number % 4 == 0, named(crowded, number // 4), named(usual, number - number // 4 - 1))
    mixed = jax.random.permutation(jax.random.fold_in(own, 3), number_of)
    source_of, taker = mixed[0:number_of // 2 * 2:2], mixed[1:number_of // 2 * 2:2]
    slack = jnp.minimum(lengths[source_of] - 1, bound - lengths[taker]) // 2
    slack = jnp.where((source_of == sequence[0]) | (taker == sequence[0]) | (lengths[taker] == 0), 0, jnp.maximum(slack, 0))
    shifted = jax.random.randint(jax.random.fold_in(own, 4), (number_of // 2,), 0, 1 << 20) % (slack + 1)
    lengths = lengths.at[source_of].add(-shifted).at[taker].add(shifted)
    labels = jnp.searchsorted(jnp.cumsum(lengths), jnp.arange(rows * top), side="right").astype(jnp.int32)
    listing = labels.reshape(top, rows).T
    listing = listing[jax.random.permutation(jax.random.fold_in(own, 1), rows)]
    rotation = jax.random.randint(jax.random.fold_in(own, 2), (rows, 1), 0, top)
    return jnp.take_along_axis(listing, (jnp.arange(top)[None, :] + rotation) % top, axis=1)


def load_shares(number_of, total, limit, slope, full):
    loads = [(1 << 20) // math.isqrt(rank ** slope) + 1 for rank in range(1, number_of + 1)]
    largest = limit if full else min(limit, max(-(-total // number_of), total * loads[0] // sum(loads)))
    least = 1 if total - largest >= number_of - 1 else 0
    holding, spare = [largest] + [least] * (number_of - 1), total - largest - least * (number_of - 1)
    while spare > 0:
        movable = [i for i in range(1, number_of) if holding[i] < largest] or [i for i in range(1, number_of) if holding[i] < limit]
        whole, left = sum([loads[i] for i in movable]), spare
        for i in movable:
            more = min(limit - holding[i], max(1, left * loads[i] // whole), spare)
            holding[i] = holding[i] + more
            spare = spare - more
    return np.array(holding)


def gaussian(own_key, shape, scale, most, pieces=(), kind=jnp.bfloat16):
    level = block_levels(own_key, shape, pieces, -0.22, 0.18) if pieces else 1.0
    entries = jax.random.normal(own_key, shape, jnp.float32) * scale * level
    return jnp.minimum(jnp.maximum(entries, -most), most).astype(kind)


def setup_inputs(seed: int = 0) -> dict:
    arg_keys = jax.random.split(jax.random.key(seed), 13)
    initial_state = gaussian(arg_keys[0], (ENS, NLAT, NLON, C), 1.0, 6.0, ((0, 2), (1, 4), (2, 4)))
    background = gaussian(arg_keys[1], (ENS, NLAT, NLON, C), 1.0, 6.0, ((0, 2), (1, 4), (2, 4)))
    background_precision = jnp.clip(jnp.exp(jax.random.uniform(arg_keys[2], (C,), jnp.float32, math.log(0.5), math.log(4.0))), 0.5, 4.0)
    kernel_taps = gaussian(arg_keys[3], (LAYERS, KERNEL, C), 0.2, 1.0, (), jnp.float32)
    norm_gains = jnp.clip(jnp.exp(jax.random.uniform(arg_keys[4], (LAYERS, C), jnp.float32, math.log(0.5), math.log(2.0))), 0.5, 2.0)
    weight_in = gaussian(arg_keys[5], (LAYERS, C, HID), C ** -0.5, 0.375)
    weight_out = gaussian(arg_keys[6], (LAYERS, HID, C), HID ** -0.5, 0.25)
    obs_operator = gaussian(arg_keys[7], (C, K), C ** -0.5, 0.375)
    obs_precision = jnp.clip(jnp.exp(jax.random.uniform(arg_keys[8], (K,), jnp.float32, math.log(0.5), math.log(4.0))), 0.5, 4.0)
    obs_values = gaussian(arg_keys[9], (OBS, K), 1.0, 6.0, ((0, 16),))
    obs_owner_keys = jax.random.split(jax.random.fold_in(arg_keys[10], 1), OBS // OBS_DEV)
    obs_owner_turns = jax.random.permutation(jax.random.fold_in(arg_keys[10], 3), OBS // OBS_DEV)
    obs_owner = jax.vmap(lambda own, number: assign_block(jax.random.fold_in(arg_keys[10], 2), own, number, OBS_DEV, NGRID, 1, CAP, 2))(obs_owner_keys, obs_owner_turns).reshape((OBS, 1))
    obs_cell = place_ends(jax.random.randint(arg_keys[11], (OBS,), 0, CLAT * CLON), jax.random.fold_in(arg_keys[11], 1), 0, (CLAT * CLON) - 1).astype(jnp.int32)
    return {"initial_state": initial_state, "background": background, "background_precision": background_precision, "kernel_taps": kernel_taps, "norm_gains": norm_gains, "weight_in": weight_in, "weight_out": weight_out, "obs_operator": obs_operator, "obs_precision": obs_precision, "obs_values": obs_values, "obs_owner": obs_owner, "obs_cell": obs_cell}


SQRT_TWO_OVER_PI = 0.7978845608
CUBIC = 0.044715
EPSILON = 1e-06

def gelu_value(values):
    return 0.5 * values * (1.0 + jnp.tanh(SQRT_TWO_OVER_PI * (values + CUBIC * values * values * values)))

def gelu_slope(values):
    inner = jnp.tanh(SQRT_TWO_OVER_PI * (values + CUBIC * values * values * values))
    return 0.5 * (1.0 + inner) + 0.5 * values * (1.0 - inner * inner) * SQRT_TWO_OVER_PI * (1.0 + 3.0 * CUBIC * values * values)

def pad_grid(field):
    padded = jnp.pad(field, ((2, 2), (0, 0), (0, 0)))
    return jnp.concatenate([padded[:, -2:], padded, padded[:, :2]], axis=1)

def depthwise(padded, kernel, height, width):
    summed = jnp.zeros((height, width, padded.shape[2]), jnp.float32)
    for row_tap in range(5):
        for col_tap in range(5):
            summed = summed + kernel[5 * row_tap + col_tap] * padded[row_tap:row_tap + height, col_tap:col_tap + width].astype(jnp.float32)
    return summed

def transposed(padded, kernel, height, width):
    summed = jnp.zeros((height, width, padded.shape[2]), jnp.float32)
    for row_tap in range(5):
        for col_tap in range(5):
            summed = summed + kernel[5 * row_tap + col_tap] * padded[4 - row_tap:4 - row_tap + height, 4 - col_tap:4 - col_tap + width].astype(jnp.float32)
    return summed

def front_part(conv_out, gain_row, layer_in, layer_out):
    channels = conv_out.shape[-1]
    flat_conv = conv_out.reshape(-1, channels)
    inverse_rms = lax.rsqrt(lax.optimization_barrier(jnp.mean(flat_conv * flat_conv, axis=1, keepdims=True)) + EPSILON)
    normed = (flat_conv * inverse_rms * gain_row).astype(jnp.bfloat16)
    hidden = jnp.dot(normed, layer_in, preferred_element_type=jnp.float32)
    active = gelu_value(hidden).astype(jnp.bfloat16)
    mixed = jnp.dot(active, layer_out, preferred_element_type=jnp.float32)
    return (mixed.reshape(conv_out.shape), hidden)

def back_part(conv_out, upstream, gain_row, layer_in, layer_out):
    channels = conv_out.shape[-1]
    flat_conv = conv_out.reshape(-1, channels)
    inverse_rms = lax.rsqrt(lax.optimization_barrier(jnp.mean(flat_conv * flat_conv, axis=1, keepdims=True)) + EPSILON)
    normed = (flat_conv * inverse_rms * gain_row).astype(jnp.bfloat16)
    hidden = jnp.dot(normed, layer_in, preferred_element_type=jnp.float32)
    back_hidden = jnp.dot(upstream.reshape(-1, channels).astype(jnp.bfloat16), layer_out.T, preferred_element_type=jnp.float32)
    hidden_grad = (back_hidden * gelu_slope(hidden)).astype(jnp.bfloat16)
    normed_grad = jnp.dot(hidden_grad, layer_in.T, preferred_element_type=jnp.float32)
    weighted = normed_grad * gain_row
    cube = inverse_rms * inverse_rms * inverse_rms
    conv_grad = inverse_rms * weighted - flat_conv * cube * lax.optimization_barrier(jnp.mean(weighted * flat_conv, axis=1, keepdims=True))
    return conv_grad.astype(jnp.bfloat16).reshape(conv_out.shape)

def forward_layer(model_state, kernel, gain_row, layer_in, layer_out):
    padded = pad_grid(model_state)
    width = model_state.shape[1]
    blocks = model_state.shape[0] // CLAT

    def one_block(block_index):
        row_slab = lax.dynamic_slice_in_dim(padded, block_index * CLAT, CLAT + 4, 0)
        conv_out = depthwise(row_slab, kernel, CLAT, width)
        residual = lax.dynamic_slice_in_dim(model_state, block_index * CLAT, CLAT, 0).astype(jnp.float32)
        mixed, hidden = front_part(conv_out, gain_row, layer_in, layer_out)
        return (residual + mixed).astype(jnp.bfloat16)
    result = lax.map(one_block, jnp.arange(blocks, dtype=jnp.int32))
    return result.reshape(model_state.shape)

def adjoint_layer(model_state, upstream, kernel, gain_row, layer_in, layer_out):
    padded = pad_grid(model_state)
    width = model_state.shape[1]
    blocks = model_state.shape[0] // CLAT

    def norm_block(block_index):
        row_slab = lax.dynamic_slice_in_dim(padded, block_index * CLAT, CLAT + 4, 0)
        conv_out = depthwise(row_slab, kernel, CLAT, width)
        incoming = lax.dynamic_slice_in_dim(upstream, block_index * CLAT, CLAT, 0)
        return back_part(conv_out, incoming, gain_row, layer_in, layer_out)
    conv_grad = lax.map(norm_block, jnp.arange(blocks, dtype=jnp.int32)).reshape(model_state.shape)
    grad_padded = pad_grid(conv_grad)

    def spread_block(block_index):
        row_slab = lax.dynamic_slice_in_dim(grad_padded, block_index * CLAT, CLAT + 4, 0)
        incoming = lax.dynamic_slice_in_dim(upstream, block_index * CLAT, CLAT, 0)
        return incoming + transposed(row_slab, kernel, CLAT, width)
    result = lax.map(spread_block, jnp.arange(blocks, dtype=jnp.int32))
    return result.reshape(model_state.shape)

def reference(initial_state, background, background_precision, kernel_taps, norm_gains, weight_in, weight_out, obs_operator, obs_precision, obs_values, obs_owner, obs_cell):
    members = initial_state.shape[0]
    owner_ids = obs_owner[:, 0]
    lat_row = (owner_ids // N_LON * CLAT + obs_cell // CLON).astype(jnp.int32)
    lon_col = (owner_ids % N_LON * CLON + obs_cell % CLON).astype(jnp.int32)
    summed = jnp.zeros((obs_values.shape[0], obs_values.shape[1]), jnp.float32)
    middles = []
    for member in range(members):
        start_state = initial_state[member]
        middle = forward_layer(start_state, kernel_taps[0], norm_gains[0], weight_in[0], weight_out[0])
        final_state = forward_layer(middle, kernel_taps[1], norm_gains[1], weight_in[1], weight_out[1])
        state_rows = final_state[lat_row, lon_col]
        summed = summed + jnp.dot(state_rows, obs_operator, preferred_element_type=jnp.float32)
        middles.append(middle)
    mean_pred = summed / members
    obs_adjoint = (obs_precision * (mean_pred - obs_values.astype(jnp.float32)) / members).astype(jnp.bfloat16)
    spread = jnp.dot(obs_adjoint, obs_operator.T, preferred_element_type=jnp.float32)
    grid_shape = (initial_state.shape[1], initial_state.shape[2], initial_state.shape[3])
    last_grad = jnp.zeros(grid_shape, jnp.float32).at[lat_row, lon_col].add(spread)
    gradients = []
    for member in range(members):
        start_state = initial_state[member]
        middle_grad = adjoint_layer(middles[member], last_grad, kernel_taps[1], norm_gains[1], weight_in[1], weight_out[1])
        start_grad = adjoint_layer(start_state, middle_grad, kernel_taps[0], norm_gains[0], weight_in[0], weight_out[0])
        prior = background_precision * (start_state.astype(jnp.float32) - background[member].astype(jnp.float32))
        gradients.append(prior + start_grad)
    return jnp.stack(gradients)
```

```python
import functools

import jax
import jax.numpy as jnp
from jax import lax
from jax.experimental import pallas as pl
from jax.experimental.pallas import tpu as pltpu
from jax.sharding import PartitionSpec as P

SQRT_TWO_OVER_PI = 0.7978845608
CUBIC = 0.044715
EPSILON = 1e-06
LANES = 128
ROWS = 8
VMEM_BYTES = 56 * 1024 * 1024


def dot(a, b):
    return jnp.dot(a, b, preferred_element_type=jnp.float32)


def dot_t(a, b):
    return lax.dot_general(a, b, (((1,), (1,)), ((), ())), preferred_element_type=jnp.float32)


def shifted_copies(x, up, down, left, right, xp, xs):
    height, width, _ = x.shape
    xp[0:2, 8 : 8 + width] = up[...].astype(jnp.float32)
    xp[height + 2 : height + 4, 8 : 8 + width] = down[...].astype(jnp.float32)
    xp[:, 6:8] = left[...].astype(jnp.float32)
    xp[:, 8 + width : 10 + width] = right[...].astype(jnp.float32)

    def fill(step, carry):
        r = step * 4
        xp[pl.ds(r + 2, 4), 8 : 8 + width] = x[pl.ds(r, 4)].astype(jnp.float32)
        return carry

    lax.fori_loop(0, height // 4, fill, 0)

    def shift(step, carry):
        r = step * 4
        for j in range(5):
            xs[j, pl.ds(r, 4)] = xp[pl.ds(r, 4), 6 + j : 6 + j + width]
        return carry

    lax.fori_loop(0, (height + 4) // 4, shift, 0)


def conv_rows(xs, taps, out, r0):
    width, channels = xs.shape[2], xs.shape[3]

    def column(step, carry):
        c0 = pl.multiple_of(step * 8, 8)
        for part in range(channels // LANES):
            lanes = slice(part * LANES, (part + 1) * LANES)
            acc = None
            for j in range(5):
                xj = xs[j, pl.ds(r0, ROWS + 4), pl.ds(c0, 8), lanes]
                for i in range(5):
                    tap = taps[5 * i + j : 5 * i + j + 1, lanes][None]
                    term = tap * xj[i : i + ROWS]
                    acc = term if acc is None else acc + term
            out[:, pl.ds(c0, 8), lanes] = acc
        return carry

    lax.fori_loop(0, width // 8, column, 0)


def forward_block(h, x, gain, w_in, w_out):
    s = lax.rsqrt(jnp.mean(h * h, axis=1, keepdims=True) + EPSILON)
    n = (h * s * gain).astype(jnp.bfloat16)
    z = dot(n, w_in)
    zz = z * z
    inner = jnp.tanh(z * (SQRT_TWO_OVER_PI + (SQRT_TWO_OVER_PI * CUBIC) * zz))
    half = 0.5 + 0.5 * inner
    t = (z * half).astype(jnp.bfloat16)
    slope = half + (z * (0.5 - 0.5 * inner * inner)) * (
        SQRT_TWO_OVER_PI + (SQRT_TWO_OVER_PI * 3.0 * CUBIC) * zz
    )
    mixed = dot(t, w_out)
    return s, n, slope.astype(jnp.bfloat16), (x.astype(jnp.float32) + mixed).astype(jnp.bfloat16)


def backward_block(g, n, s, slope, gain, w_in, w_out):
    u = dot_t(g.astype(jnp.bfloat16), w_out)
    dz = (u * slope.astype(jnp.float32)).astype(jnp.bfloat16)
    dn = dot_t(dz, w_in)
    nf = n.astype(jnp.float32)
    m = jnp.mean(dn * nf, axis=1, keepdims=True)
    return (s * (gain * dn - (nf * (1.0 / gain)) * m)).astype(jnp.bfloat16)


def forward_layer(x, up, down, left, right, taps, gain, w_in, w_out, nxt, n_out, s_out, slope_out, xp, xs, hb):
    height, width, channels = x.shape
    shifted_copies(x, up, down, left, right, xp, xs)

    def block(step, carry):
        r0 = step * ROWS
        conv_rows(xs, taps, hb, r0)
        cells = ROWS * width
        flat = pl.ds(pl.multiple_of(step * cells, cells), cells)
        s, n, slope, new = forward_block(
            hb[...].reshape(cells, channels),
            x[pl.ds(r0, ROWS)].reshape(cells, channels),
            gain[...],
            w_in[...],
            w_out[...],
        )
        nxt[pl.ds(r0, ROWS)] = new.reshape(ROWS, width, channels)
        n_out[flat] = n
        s_out[flat] = jnp.broadcast_to(s, (cells, LANES))
        slope_out[flat] = slope
        return carry

    lax.fori_loop(0, height // ROWS, block, 0)


def first_kernel(*refs):
    forward_layer(*refs)


def second_kernel(x, up, down, left, right, taps, gain, w_in, w_out, cells_col, op, n_out, s_out, slope_out, pred, xp, xs, hb, last):
    forward_layer(x, up, down, left, right, taps, gain, w_in, w_out, last, n_out, s_out, slope_out, xp, xs, hb)
    height, width, channels = x.shape
    cells = height * width
    chunk = 256
    state = last[...].reshape(cells, channels)

    def gather(step, carry):
        at = pl.ds(pl.multiple_of(step * chunk, chunk), chunk)
        where = lax.broadcasted_iota(jnp.int32, (chunk, cells), 1)
        hot = (where == cells_col[at]).astype(jnp.float32).astype(jnp.bfloat16)
        rows = dot(hot, state).astype(jnp.bfloat16)
        pred[at] = dot(rows, op[...])
        return carry

    lax.fori_loop(0, cells_col.shape[0] // chunk, gather, 0)


def adjoint_kernel(members, mine, other, values, cells_row, op, precision, n_in, s_in, slope_in, gain, w_in, w_out, g_out, dh_out):
    width = dh_out.shape[1]
    slots = mine.shape[0]
    mean_pred = (mine[...] + other[...]) * (1.0 / members)
    adj = (precision[...] * (mean_pred - values[...].astype(jnp.float32)) * (1.0 / members)).astype(jnp.bfloat16)
    cells = ROWS * width

    def block(step, carry):
        flat = pl.ds(pl.multiple_of(step * cells, cells), cells)
        where = lax.broadcasted_iota(jnp.int32, (cells, slots), 0) + step * cells
        hot = (where == cells_row[...]).astype(jnp.float32).astype(jnp.bfloat16)
        total = dot(hot, adj)
        high = total.astype(jnp.bfloat16)
        low = (total - high.astype(jnp.float32)).astype(jnp.bfloat16)
        g = dot_t(high, op[...]) + dot_t(low, op[...])
        g_out[flat] = g
        dh = backward_block(
            g, n_in[flat], s_in[flat][:, 0:1], slope_in[flat], gain[...], w_in[...], w_out[...]
        )
        dh_out[pl.ds(step * ROWS, ROWS)] = dh.reshape(ROWS, width, dh.shape[1])
        return carry

    lax.fori_loop(0, dh_out.shape[0] // ROWS, block, 0)


def middle_kernel(dh, up, down, left, right, taps, g_in, n_in, s_in, slope_in, gain, w_in, w_out, g_out, dh_out, xp, xs, hb):
    height, width, channels = dh.shape
    shifted_copies(dh, up, down, left, right, xp, xs)
    cells = ROWS * width

    def block(step, carry):
        r0 = step * ROWS
        conv_rows(xs, taps, hb, r0)
        flat = pl.ds(pl.multiple_of(step * cells, cells), cells)
        g = g_in[flat] + hb[...].reshape(cells, channels)
        g_out[flat] = g
        new = backward_block(
            g, n_in[flat], s_in[flat][:, 0:1], slope_in[flat], gain[...], w_in[...], w_out[...]
        )
        dh_out[pl.ds(r0, ROWS)] = new.reshape(ROWS, width, channels)
        return carry

    lax.fori_loop(0, height // ROWS, block, 0)


def last_kernel(dh, up, down, left, right, taps, g_in, x, background, precision, out, xp, xs, hb):
    height, width, channels = dh.shape
    shifted_copies(dh, up, down, left, right, xp, xs)
    cells = ROWS * width

    def block(step, carry):
        r0 = step * ROWS
        conv_rows(xs, taps, hb, r0)
        flat = pl.ds(pl.multiple_of(step * cells, cells), cells)
        rows = pl.ds(r0, ROWS)
        diff = x[rows].astype(jnp.float32) - background[rows].astype(jnp.float32)
        prior = precision[...] * diff.reshape(cells, channels)
        out[rows] = (prior + (g_in[flat] + hb[...].reshape(cells, channels))).reshape(ROWS, width, channels)
        return carry

    lax.fori_loop(0, height // ROWS, block, 0)


def call(kernel, outs, args, scratch=(), flops=0):
    whole = pl.BlockSpec(memory_space=pltpu.VMEM)
    moved = sum(a.size * a.dtype.itemsize for a in args) + sum(o.size * o.dtype.itemsize for o in outs)
    return pl.pallas_call(
        kernel,
        out_shape=list(outs),
        in_specs=[whole] * len(args),
        out_specs=[whole] * len(outs),
        scratch_shapes=list(scratch),
        compiler_params=pltpu.CompilerParams(vmem_limit_bytes=VMEM_BYTES),
        cost_estimate=pl.CostEstimate(flops=flops, bytes_accessed=moved, transcendentals=0),
    )(*args)


def halos(field):
    height, width, _ = field.shape
    lat = lax.axis_size("lat")
    lon = lax.axis_size("lon")
    up_perm = [(i, i + 1) for i in range(lat - 1)]
    down_perm = [(i + 1, i) for i in range(lat - 1)]
    up = lax.ppermute(field[height - 2 :], "lat", up_perm)
    down = lax.ppermute(field[:2], "lat", down_perm)
    right_edge = jnp.concatenate([up[:, width - 2 :], field[:, width - 2 :], down[:, width - 2 :]], axis=0)
    left_edge = jnp.concatenate([up[:, :2], field[:, :2], down[:, :2]], axis=0)
    left = lax.ppermute(right_edge, "lon", [(i, (i + 1) % lon) for i in range(lon)])
    right = lax.ppermute(left_edge, "lon", [((i + 1) % lon, i) for i in range(lon)])
    return up, down, left, right


def route(obs_values, obs_owner, obs_cell, grid_count, capacity):
    count, channels = obs_values.shape
    bf16 = jnp.bfloat16
    owner = obs_owner[:, 0]
    hits = owner[:, None] == jnp.arange(grid_count, dtype=jnp.int32)[None, :]
    order = jnp.arange(count, dtype=jnp.int32)
    earlier = dot((order[None, :] < order[:, None]).astype(bf16), hits.astype(bf16))
    rank = jnp.sum(jnp.where(hits, earlier, 0.0), axis=1).astype(jnp.int32)
    slot = owner * capacity + rank
    slots = grid_count * capacity
    hot = (jnp.arange(slots, dtype=jnp.int32)[:, None] == slot[None, :]).astype(bf16)
    send_values = dot(hot, obs_values).astype(bf16)
    cell_parts = jnp.stack([obs_cell // 64, obs_cell % 64, jnp.ones_like(obs_cell)], axis=1).astype(bf16)
    parts = dot(hot, cell_parts).astype(jnp.int32)
    send_cells = parts[:, 0] * 64 + parts[:, 1] + parts[:, 2] - 1
    axes = ("lat", "lon")
    values = lax.all_to_all(
        send_values.reshape(grid_count, capacity, channels), axes, split_axis=0, concat_axis=0, tiled=True
    )
    cells = lax.all_to_all(
        send_cells.reshape(grid_count, capacity), axes, split_axis=0, concat_axis=0, tiled=True
    )
    return values.reshape(slots, channels), cells.reshape(slots)


def per_device(
    initial_state,
    background,
    background_precision,
    kernel_taps,
    norm_gains,
    weight_in,
    weight_out,
    obs_operator,
    obs_precision,
    obs_values,
    obs_owner,
    obs_cell,
):
    f32, bf16 = jnp.float32, jnp.bfloat16
    shape = jax.ShapeDtypeStruct
    start = initial_state[0]
    height, width, channels = start.shape
    hidden = weight_in.shape[2]
    cells = height * width
    obs_channels = obs_values.shape[1]
    members = lax.axis_size("ens")
    grid_count = lax.axis_size("lat") * lax.axis_size("lon")
    capacity = 2 * obs_values.shape[0] // grid_count
    slots = grid_count * capacity
    values, got_cells = route(obs_values, obs_owner, obs_cell, grid_count, capacity)

    conv_scratch = [
        pltpu.VMEM((height + 4, width + 16, channels), f32),
        pltpu.VMEM((5, height + 4, width, channels), f32),
        pltpu.VMEM((ROWS, width, channels), f32),
    ]
    state_shape = shape((height, width, channels), bf16)
    kept = [shape((cells, channels), bf16), shape((cells, LANES), f32), shape((cells, hidden), bf16)]
    conv_flops = 50 * cells * channels
    mix_flops = 4 * cells * channels * hidden
    gains = norm_gains[:, None, :]
    reverse = kernel_taps[:, ::-1]

    middle, n1, s1, slope1 = call(
        first_kernel,
        [state_shape] + kept,
        [start, *halos(start), kernel_taps[0], gains[0], weight_in[0], weight_out[0]],
        conv_scratch,
        conv_flops + mix_flops,
    )
    n2, s2, slope2, pred = call(
        second_kernel,
        kept + [shape((slots, obs_channels), f32)],
        [middle, *halos(middle), kernel_taps[1], gains[1], weight_in[1], weight_out[1], got_cells[:, None], obs_operator],
        conv_scratch + [pltpu.VMEM((height, width, channels), bf16)],
        conv_flops + mix_flops,
    )
    if members == 2:
        other = lax.ppermute(pred, "ens", [(0, 1), (1, 0)])
    else:
        other = lax.psum(pred, "ens") - pred
    g2, dh2 = call(
        functools.partial(adjoint_kernel, members),
        [shape((cells, channels), f32), state_shape],
        [pred, other, values, got_cells[None, :], obs_operator, obs_precision[None, :], n2, s2, slope2, gains[1], weight_in[1], weight_out[1]],
        (),
        mix_flops,
    )
    g1, dh1 = call(
        middle_kernel,
        [shape((cells, channels), f32), state_shape],
        [dh2, *halos(dh2), reverse[1], g2, n1, s1, slope1, gains[0], weight_in[0], weight_out[0]],
        conv_scratch,
        conv_flops + mix_flops,
    )
    (out,) = call(
        last_kernel,
        [shape((height, width, channels), f32)],
        [dh1, *halos(dh1), reverse[0], g1, start, background[0], background_precision[None, :]],
        conv_scratch,
        conv_flops,
    )
    return out[None]


def solution(mesh):
    in_specs = (
        P("ens", "lat", "lon", None),
        P("ens", "lat", "lon", None),
        P(),
        P(),
        P(),
        P(),
        P(),
        P(),
        P(),
        P(("lat", "lon"), None),
        P(("lat", "lon"), None),
        P(("lat", "lon")),
    )
    out_specs = P("ens", "lat", "lon", None)
    return jax.shard_map(
        per_device, mesh=mesh, in_specs=in_specs, out_specs=out_specs, check_vma=False
    )
```

```python
import functools

import jax
import jax.numpy as jnp
from jax import lax
from jax.experimental import pallas as pl
from jax.experimental.pallas import tpu as pltpu
from jax.sharding import PartitionSpec as P

SQRT_TWO_OVER_PI = 0.7978845608
CUBIC = 0.044715
EPSILON = 1e-06
LANES = 128
ROWS = 8
VMEM_BYTES = 56 * 1024 * 1024


def dot(a, b):
    return jnp.dot(a, b, preferred_element_type=jnp.float32)


def dot_t(a, b):
    return lax.dot_general(a, b, (((1,), (1,)), ((), ())), preferred_element_type=jnp.float32)


DIRECTIONS = ((-1, 0), (1, 0), (0, -1), (0, 1), (-1, -1), (-1, 1), (1, -1), (1, 1))
MESH = pl.DeviceIdType.MESH


def conv_rows(xs, taps, out, r0, flip):
    width, channels = xs.shape[2], xs.shape[3]

    def column(step, carry):
        c0 = pl.multiple_of(step * 8, 8)
        for part in range(channels // LANES):
            lanes = slice(part * LANES, (part + 1) * LANES)
            acc = None
            for j in range(5):
                xj = xs[j, pl.ds(r0, ROWS + 4), pl.ds(c0, 8), lanes]
                for i in range(5):
                    at = 24 - (5 * i + j) if flip else 5 * i + j
                    term = taps[at : at + 1, lanes][None] * xj[i : i + ROWS]
                    acc = term if acc is None else acc + term
            out[:, pl.ds(c0, 8), lanes] = acc
        return carry

    lax.fori_loop(0, width // 8, column, 0)


def forward_block(h, x, gain, w_in, w_out):
    s = lax.rsqrt(jnp.mean(h * h, axis=1, keepdims=True) + EPSILON)
    n = (h * s * gain).astype(jnp.bfloat16)
    z = dot(n, w_in)
    zz = z * z
    inner = jnp.tanh(z * (SQRT_TWO_OVER_PI + (SQRT_TWO_OVER_PI * CUBIC) * zz))
    half = 0.5 + 0.5 * inner
    t = (z * half).astype(jnp.bfloat16)
    slope = half + (z * (0.5 - 0.5 * inner * inner)) * (
        SQRT_TWO_OVER_PI + (SQRT_TWO_OVER_PI * 3.0 * CUBIC) * zz
    )
    mixed = dot(t, w_out)
    return s, n, slope.astype(jnp.bfloat16), (x.astype(jnp.float32) + mixed).astype(jnp.bfloat16)


def backward_block(g, n, s, slope, gain, w_in, w_out):
    u = dot_t(g.astype(jnp.bfloat16), w_out)
    dz = (u * slope.astype(jnp.float32)).astype(jnp.bfloat16)
    dn = dot_t(dz, w_in)
    nf = n.astype(jnp.float32)
    m = jnp.mean(dn * nf, axis=1, keepdims=True)
    return (s * (gain * dn - (nf * (1.0 / gain)) * m)).astype(jnp.bfloat16)


def kernel(
    mesh_shape,
    x,
    background,
    prior_precision,
    taps,
    gains,
    w_in,
    w_out,
    op,
    precision,
    obs_values,
    owner,
    cell,
    out,
    middle,
    last,
    cotangent,
    grad,
    n_keep,
    s_keep,
    slope_keep,
    xp,
    xs,
    hb,
    stage_side,
    stage_corner,
    got_edge,
    got_side,
    got_corner,
    outbox,
    inbox,
    mine,
    other,
    halo_send,
    halo_recv,
    box_send,
    box_recv,
    ens_send,
    ens_recv,
):
    f32, bf16 = jnp.float32, jnp.bfloat16
    lats, lons, members = mesh_shape
    height, width, channels = x.shape
    lat, lon, ens = lax.axis_index("lat"), lax.axis_index("lon"), lax.axis_index("ens")
    grid = lats * lons
    me = lat * lons + lon
    slots = inbox.shape[0]
    capacity = slots // grid
    partner = {"lat": lat, "lon": lon, "ens": 1 - ens}
    cells = ROWS * width

    def peer(k):
        to = lax.rem(me + k, grid)
        return {"lat": to // lons, "lon": lax.rem(to, lons), "ens": ens}

    barrier = pltpu.get_barrier_semaphore()

    def greet(k, carry):
        pl.semaphore_signal(barrier, inc=1, device_id=peer(k), device_id_type=MESH)
        return carry

    lax.fori_loop(1, grid, greet, 0)
    pl.semaphore_signal(barrier, inc=1, device_id=partner, device_id_type=MESH)
    pl.semaphore_wait(barrier, grid)

    def send(step, field):
        def fill(k, carry):
            r = k * 4
            xp[pl.ds(r + 2, 4), 8 : 8 + width] = field[pl.ds(r, 4)].astype(f32)
            return carry

        lax.fori_loop(0, height // 4, fill, 0)
        for side, first in ((0, 8), (1, 6 + width)):
            for c in range(2):
                stage_side[step, side, c * height : (c + 1) * height] = xp[2 : 2 + height, first + c, :]
        for k, (down, east) in enumerate(DIRECTIONS[4:]):
            r0 = 2 if down < 0 else height
            c0 = 8 if east < 0 else 6 + width
            for r in range(2):
                stage_corner[step, k, 4 * r : 4 * r + 2] = xp[r0 + r, c0 : c0 + 2, :]
        copies = []
        for d, (down, east) in enumerate(DIRECTIONS):
            if d < 2:
                source = field.at[0:2] if down < 0 else field.at[height - 2 : height]
                target = got_edge.at[step, d]
            elif d < 4:
                source, target = stage_side.at[step, d - 2], got_side.at[step, d - 2]
            else:
                source, target = stage_corner.at[step, d - 4], got_corner.at[step, d - 4]
            copy = pltpu.make_async_remote_copy(
                src_ref=source,
                dst_ref=target,
                send_sem=halo_send.at[step, d],
                recv_sem=halo_recv.at[step, d],
                device_id={
                    "lat": lax.rem(lat + down + lats, lats),
                    "lon": lax.rem(lon + east + lons, lons),
                    "ens": ens,
                },
                device_id_type=MESH,
            )
            copy.start()
            copies.append(copy)
        return copies

    def receive(step, copies):
        for copy in copies:
            copy.wait()
        above = (lat > 0).astype(f32)
        below = (lat < lats - 1).astype(f32)
        xp[height + 2 : height + 4, 8 : 8 + width] = got_edge[step, 0].astype(f32) * below
        xp[0:2, 8 : 8 + width] = got_edge[step, 1].astype(f32) * above
        for side, first in ((0, 8 + width), (1, 6)):
            for c in range(2):
                xp[2 : 2 + height, first + c, :] = got_side[step, side, c * height : (c + 1) * height]
        for k, (down, east) in enumerate(DIRECTIONS[4:]):
            r0, keep = (height + 2, below) if down < 0 else (0, above)
            c0 = 8 + width if east < 0 else 6
            for r in range(2):
                xp[r0 + r, c0 : c0 + 2, :] = got_corner[step, k, 4 * r : 4 * r + 2] * keep

        def shift(k, carry):
            r = k * 4
            for j in range(5):
                xs[j, pl.ds(r, 4)] = xp[pl.ds(r, 4), 6 + j : 6 + j + width]
            return carry

        lax.fori_loop(0, (height + 4) // 4, shift, 0)

    def flat_rows(k):
        return pl.ds(pl.multiple_of(k * cells, cells), cells)

    def forward(layer, field, new_field):
        def block(k, carry):
            rows = pl.ds(k * ROWS, ROWS)
            conv_rows(xs, taps.at[layer], hb, k * ROWS, False)
            s, n, slope, new = forward_block(
                hb[...].reshape(cells, channels),
                field[rows].reshape(cells, channels),
                gains[layer : layer + 1],
                w_in[layer],
                w_out[layer],
            )
            new_field[rows] = new.reshape(ROWS, width, channels)
            n_keep[layer, flat_rows(k)] = n
            s_keep[layer, flat_rows(k)] = jnp.broadcast_to(s, (cells, LANES))
            slope_keep[layer, flat_rows(k)] = slope
            return carry

        lax.fori_loop(0, height // ROWS, block, 0)

    def backward(layer, k, g, slot):
        flat = flat_rows(k)
        dh = backward_block(
            g,
            n_keep[layer, flat],
            s_keep[layer, flat][:, 0:1],
            slope_keep[layer, flat],
            gains[layer : layer + 1],
            w_in[layer],
            w_out[layer],
        )
        cotangent[slot, pl.ds(k * ROWS, ROWS)] = dh.reshape(ROWS, width, channels)

    copies = send(0, x)

    count, obs_channels = obs_values.shape
    hits = owner[...] == lax.broadcasted_iota(jnp.int32, (count, LANES), 1)
    hits = hits.astype(f32)
    order = lax.broadcasted_iota(jnp.int32, (count, count), 1)
    place = lax.broadcasted_iota(jnp.int32, (count, count), 0)
    earlier = dot((order < place).astype(f32).astype(bf16), hits.astype(bf16))
    rank = jnp.sum(hits * earlier, axis=1, keepdims=True).astype(jnp.int32)
    slot = owner[...] * capacity + rank
    hot = (lax.broadcasted_iota(jnp.int32, (count, slots), 1) == slot).astype(f32).astype(bf16)
    lane = lax.broadcasted_iota(jnp.int32, (count, LANES), 1)
    parts = jnp.where(lane == 0, cell[...] // 64, jnp.where(lane == 1, cell[...] % 64, jnp.where(lane == 2, 1, 0)))
    content = jnp.concatenate([obs_values[...], parts.astype(f32).astype(bf16)], axis=1)
    outbox[...] = lax.dot_general(
        hot, content, (((0,), (0,)), ((), ())), preferred_element_type=f32
    ).astype(outbox.dtype)

    def box(k):
        to = lax.rem(me + k, grid)
        return pltpu.make_async_remote_copy(
            src_ref=outbox.at[pl.ds(pl.multiple_of(to * capacity, capacity), capacity)],
            dst_ref=inbox.at[pl.ds(pl.multiple_of(me * capacity, capacity), capacity)],
            send_sem=box_send.at[k],
            recv_sem=box_recv.at[k],
            device_id=peer(k),
            device_id_type=MESH,
        )

    def post(k, carry):
        box(k).start()
        return carry

    lax.fori_loop(1, grid, post, 0)
    own = pl.ds(pl.multiple_of(me * capacity, capacity), capacity)
    inbox[own] = outbox[own]

    receive(0, copies)
    forward(0, x, middle)
    copies = send(1, middle)
    receive(1, copies)
    forward(1, middle, last)

    def collect(k, carry):
        box(k).wait()
        return carry

    lax.fori_loop(1, grid, collect, 0)
    chunk = slots // 4
    state = last[...].reshape(height * width, channels)
    lane8 = lax.broadcasted_iota(jnp.int32, (LANES, LANES), 1)
    pick = jnp.where(lane8 == 0, 64.0, jnp.where(lane8 < 3, 1.0, 0.0)).astype(bf16)
    exchanges = []
    for k in range(4):
        at = slice(k * chunk, (k + 1) * chunk)
        where_from = dot_t(inbox[at, obs_channels:].astype(bf16), pick)[:, 0:1].astype(jnp.int32) - 1
        places = lax.broadcasted_iota(jnp.int32, (chunk, height * width), 1)
        chosen = (places == where_from).astype(f32).astype(bf16)
        picked = dot(chosen, state).astype(bf16)
        mine[at] = dot(picked, op[...]).astype(bf16)
        copy = pltpu.make_async_remote_copy(
            src_ref=mine.at[at],
            dst_ref=other.at[at],
            send_sem=ens_send.at[k],
            recv_sem=ens_recv.at[k],
            device_id=partner,
            device_id_type=MESH,
        )
        copy.start()
        exchanges.append(copy)
    cells_row = dot_t(pick[0:16], inbox[:, obs_channels:].astype(bf16))[0:1].astype(jnp.int32) - 1
    for copy in exchanges:
        copy.wait()
    mean_pred = (mine[...].astype(f32) + other[...].astype(f32)) * (1.0 / members)
    misfit = mean_pred - inbox[:, 0:obs_channels].astype(f32)
    adj = (precision[...] * misfit * (1.0 / members)).astype(bf16)

    def spread(k, carry):
        places = lax.broadcasted_iota(jnp.int32, (cells, slots), 0) + k * cells
        chosen = (places == cells_row).astype(f32).astype(bf16)
        total = dot(chosen, adj)
        high = total.astype(bf16)
        low = (total - high.astype(f32)).astype(bf16)
        g = dot_t(high, op[...]) + dot_t(low, op[...])
        grad[flat_rows(k)] = g
        backward(1, k, g, 0)
        return carry

    lax.fori_loop(0, height // ROWS, spread, 0)
    copies = send(2, cotangent.at[0])
    receive(2, copies)

    def inner(k, carry):
        conv_rows(xs, taps.at[1], hb, k * ROWS, True)
        g = grad[flat_rows(k)] + hb[...].reshape(cells, channels)
        grad[flat_rows(k)] = g
        backward(0, k, g, 1)
        return carry

    lax.fori_loop(0, height // ROWS, inner, 0)
    copies = send(3, cotangent.at[1])
    receive(3, copies)

    def outer(k, carry):
        rows = pl.ds(k * ROWS, ROWS)
        conv_rows(xs, taps.at[0], hb, k * ROWS, True)
        diff = x[rows].astype(f32) - background[rows].astype(f32)
        prior = prior_precision[...] * diff.reshape(cells, channels)
        total = prior + (grad[flat_rows(k)] + hb[...].reshape(cells, channels))
        out[rows] = total.reshape(ROWS, width, channels)
        return carry

    lax.fori_loop(0, height // ROWS, outer, 0)


def per_device(
    mesh_shape,
    initial_state,
    background,
    background_precision,
    kernel_taps,
    norm_gains,
    weight_in,
    weight_out,
    obs_operator,
    obs_precision,
    obs_values,
    obs_owner,
    obs_cell,
):
    f32, bf16 = jnp.float32, jnp.bfloat16
    height, width, channels = initial_state.shape[1:]
    hidden = weight_in.shape[2]
    cells = height * width
    obs_channels = obs_values.shape[1]
    grid = mesh_shape[0] * mesh_shape[1]
    capacity = 2 * obs_values.shape[0] // grid
    slots = grid * capacity
    box_type = bf16 if capacity % 16 == 0 else f32
    whole = pl.BlockSpec(memory_space=pltpu.VMEM)
    args = (
        initial_state[0],
        background[0],
        background_precision[None, :],
        kernel_taps,
        norm_gains,
        weight_in,
        weight_out,
        obs_operator,
        obs_precision[None, :],
        obs_values,
        obs_owner,
        obs_cell[:, None],
    )
    out = pl.pallas_call(
        functools.partial(kernel, mesh_shape),
        out_shape=jax.ShapeDtypeStruct((height, width, channels), f32),
        in_specs=[whole] * len(args),
        out_specs=whole,
        scratch_shapes=[
            pltpu.VMEM((height, width, channels), bf16),
            pltpu.VMEM((height, width, channels), bf16),
            pltpu.VMEM((2, height, width, channels), bf16),
            pltpu.VMEM((cells, channels), f32),
            pltpu.VMEM((2, cells, channels), bf16),
            pltpu.VMEM((2, cells, LANES), f32),
            pltpu.VMEM((2, cells, hidden), bf16),
            pltpu.VMEM((height + 4, width + 16, channels), f32),
            pltpu.VMEM((5, height + 4, width, channels), f32),
            pltpu.VMEM((ROWS, width, channels), f32),
            pltpu.VMEM((4, 2, 2 * height, channels), f32),
            pltpu.VMEM((4, 4, 8, channels), f32),
            pltpu.VMEM((4, 2, 2, width, channels), bf16),
            pltpu.VMEM((4, 2, 2 * height, channels), f32),
            pltpu.VMEM((4, 4, 8, channels), f32),
            pltpu.VMEM((slots, obs_channels + LANES), box_type),
            pltpu.VMEM((slots, obs_channels + LANES), box_type),
            pltpu.VMEM((slots, obs_channels), bf16),
            pltpu.VMEM((slots, obs_channels), bf16),
            pltpu.SemaphoreType.DMA((4, 8)),
            pltpu.SemaphoreType.DMA((4, 8)),
            pltpu.SemaphoreType.DMA((grid,)),
            pltpu.SemaphoreType.DMA((grid,)),
            pltpu.SemaphoreType.DMA((4,)),
            pltpu.SemaphoreType.DMA((4,)),
        ],
        compiler_params=pltpu.CompilerParams(
            vmem_limit_bytes=VMEM_BYTES, collective_id=0, has_side_effects=True
        ),
    )(*args)
    return out[None]


def solution(mesh):
    mesh_shape = (mesh.shape["lat"], mesh.shape["lon"], mesh.shape["ens"])
    in_specs = (
        P("ens", "lat", "lon", None),
        P("ens", "lat", "lon", None),
        P(),
        P(),
        P(),
        P(),
        P(),
        P(),
        P(),
        P(("lat", "lon"), None),
        P(("lat", "lon"), None),
        P(("lat", "lon")),
    )
    out_specs = P("ens", "lat", "lon", None)
    return jax.shard_map(
        functools.partial(per_device, mesh_shape), mesh=mesh, in_specs=in_specs, out_specs=out_specs, check_vma=False
    )
```

```python
import functools

import jax
import jax.numpy as jnp
from jax import lax
from jax.experimental import pallas as pl
from jax.experimental.pallas import tpu as pltpu
from jax.sharding import PartitionSpec as P

SQRT_TWO_OVER_PI = 0.7978845608
CUBIC = 0.044715
EPSILON = 1e-06
LANES = 128
ROWS = 8
VMEM_BYTES = 56 * 1024 * 1024


def dot(a, b):
    return jnp.dot(a, b, preferred_element_type=jnp.float32)


def dot_t(a, b):
    return lax.dot_general(a, b, (((1,), (1,)), ((), ())), preferred_element_type=jnp.float32)


DIRECTIONS = ((-1, 0), (1, 0), (0, -1), (0, 1), (-1, -1), (-1, 1), (1, -1), (1, 1))
MESH = pl.DeviceIdType.MESH


def conv_rows(xs, taps, out, r0, flip):
    width, channels = xs.shape[2], xs.shape[3]

    def column(step, carry):
        c0 = pl.multiple_of(step * 8, 8)
        for part in range(channels // LANES):
            lanes = slice(part * LANES, (part + 1) * LANES)
            acc = None
            for j in range(5):
                xj = xs[j, pl.ds(r0, ROWS + 4), pl.ds(c0, 8), lanes]
                for i in range(5):
                    at = 24 - (5 * i + j) if flip else 5 * i + j
                    term = taps[at : at + 1, lanes][None] * xj[i : i + ROWS]
                    acc = term if acc is None else acc + term
            out[:, pl.ds(c0, 8), lanes] = acc
        return carry

    lax.fori_loop(0, width // 8, column, 0, unroll=2)


def forward_block(h, x, gain, w_in, w_out):
    s = lax.rsqrt(jnp.mean(h * h, axis=1, keepdims=True) + EPSILON)
    n = (h * s * gain).astype(jnp.bfloat16)
    z = dot(n, w_in)
    zz = z * z
    inner = jnp.tanh(z * (SQRT_TWO_OVER_PI + (SQRT_TWO_OVER_PI * CUBIC) * zz))
    half = 0.5 + 0.5 * inner
    t = (z * half).astype(jnp.bfloat16)
    slope = half + (z * (0.5 - 0.5 * inner * inner)) * (
        SQRT_TWO_OVER_PI + (SQRT_TWO_OVER_PI * 3.0 * CUBIC) * zz
    )
    mixed = dot(t, w_out)
    return s, n, slope.astype(jnp.bfloat16), (x.astype(jnp.float32) + mixed).astype(jnp.bfloat16)


def backward_block(g, n, s, slope, gain, w_in, w_out):
    u = dot_t(g.astype(jnp.bfloat16), w_out)
    dz = (u * slope.astype(jnp.float32)).astype(jnp.bfloat16)
    dn = dot_t(dz, w_in)
    nf = n.astype(jnp.float32)
    m = jnp.mean(dn * nf, axis=1, keepdims=True)
    return (s * (gain * dn - (nf * (1.0 / gain)) * m)).astype(jnp.bfloat16)


def kernel(
    mesh_shape,
    x,
    background,
    prior_precision,
    taps,
    gains,
    w_in,
    w_out,
    op,
    precision,
    obs_values,
    owner,
    cell,
    out,
    middle,
    last,
    cotangent,
    grad,
    n_keep,
    s_keep,
    slope_keep,
    xp,
    xs,
    hb,
    stage_side,
    stage_corner,
    got_edge,
    got_side,
    got_corner,
    outbox,
    inbox,
    mine,
    other,
    halo_send,
    halo_recv,
    box_send,
    box_recv,
    ens_send,
    ens_recv,
):
    f32, bf16 = jnp.float32, jnp.bfloat16
    lats, lons, members = mesh_shape
    height, width, channels = x.shape
    lat, lon, ens = lax.axis_index("lat"), lax.axis_index("lon"), lax.axis_index("ens")
    grid = lats * lons
    me = lat * lons + lon
    slots = inbox.shape[0]
    capacity = slots // grid
    partner = {"lat": lat, "lon": lon, "ens": 1 - ens}
    cells = ROWS * width

    def peer(k):
        to = lax.rem(me + k, grid)
        return {"lat": to // lons, "lon": lax.rem(to, lons), "ens": ens}

    barrier = pltpu.get_barrier_semaphore()

    def greet(k, carry):
        pl.semaphore_signal(barrier, inc=1, device_id=peer(k), device_id_type=MESH)
        return carry

    lax.fori_loop(1, grid, greet, 0)
    pl.semaphore_signal(barrier, inc=1, device_id=partner, device_id_type=MESH)

    def prepare(step, field):
        def fill(k, carry):
            r = k * 4
            xp[pl.ds(r + 2, 4), 8 : 8 + width] = field[pl.ds(r, 4)].astype(f32)
            return carry

        lax.fori_loop(0, height // 4, fill, 0)
        for side, first in ((0, 8), (1, 6 + width)):
            for c in range(2):
                stage_side[step, side, c * height : (c + 1) * height] = xp[2 : 2 + height, first + c, :]
        for k, (down, east) in enumerate(DIRECTIONS[4:]):
            r0 = 2 if down < 0 else height
            c0 = 8 if east < 0 else 6 + width
            for r in range(2):
                stage_corner[step, k, 4 * r : 4 * r + 2] = xp[r0 + r, c0 : c0 + 2, :]

    def launch(step, field):
        copies = []
        for d, (down, east) in enumerate(DIRECTIONS):
            if d < 2:
                source = field.at[0:2] if down < 0 else field.at[height - 2 : height]
                target = got_edge.at[step, d]
            elif d < 4:
                source, target = stage_side.at[step, d - 2], got_side.at[step, d - 2]
            else:
                source, target = stage_corner.at[step, d - 4], got_corner.at[step, d - 4]
            copy = pltpu.make_async_remote_copy(
                src_ref=source,
                dst_ref=target,
                send_sem=halo_send.at[step, d],
                recv_sem=halo_recv.at[step, d],
                device_id={
                    "lat": lax.rem(lat + down + lats, lats),
                    "lon": lax.rem(lon + east + lons, lons),
                    "ens": ens,
                },
                device_id_type=MESH,
            )
            copy.start()
            copies.append(copy)

        def shift(k, carry):
            r = k * 4 + 2
            for j in range(5):
                xs[j, pl.ds(r, 4)] = xp[pl.ds(r, 4), 6 + j : 6 + j + width]
            return carry

        lax.fori_loop(0, height // 4, shift, 0)
        return copies

    def send(step, field):
        prepare(step, field)
        return launch(step, field)

    def receive(step, copies):
        for copy in copies:
            copy.wait()
        above = (lat > 0).astype(f32)
        below = (lat < lats - 1).astype(f32)
        xp[height + 2 : height + 4, 8 : 8 + width] = got_edge[step, 0].astype(f32) * below
        xp[0:2, 8 : 8 + width] = got_edge[step, 1].astype(f32) * above
        for side, first in ((0, 8 + width), (1, 6)):
            for c in range(2):
                xp[2 : 2 + height, first + c, :] = got_side[step, side, c * height : (c + 1) * height]
        for k, (down, east) in enumerate(DIRECTIONS[4:]):
            r0, keep = (height + 2, below) if down < 0 else (0, above)
            c0 = 8 + width if east < 0 else 6
            for r in range(2):
                xp[r0 + r, c0 : c0 + 2, :] = got_corner[step, k, 4 * r : 4 * r + 2] * keep

        for r in (0, height + 2):
            for j in range(5):
                xs[j, r : r + 2] = xp[r : r + 2, 6 + j : 6 + j + width]

        def shift(k, carry):
            rows = pl.ds(k * 8 + 2, 8)
            for j in (0, 1):
                xs[j, rows, 0:8] = xp[rows, 6 + j : 14 + j]
            for j in (3, 4):
                xs[j, rows, width - 8 : width] = xp[rows, width - 2 + j : width + 6 + j]
            return carry

        lax.fori_loop(0, height // 8, shift, 0)

    def flat_rows(k):
        return pl.ds(pl.multiple_of(k * cells, cells), cells)

    def forward(layer, field, new_field):
        def block(k, carry):
            rows = pl.ds(k * ROWS, ROWS)
            conv_rows(xs, taps.at[layer], hb, k * ROWS, False)
            s, n, slope, new = forward_block(
                hb[...].reshape(cells, channels),
                field[rows].reshape(cells, channels),
                gains[layer : layer + 1],
                w_in[layer],
                w_out[layer],
            )
            new_field[rows] = new.reshape(ROWS, width, channels)
            n_keep[layer, flat_rows(k)] = n
            s_keep[layer, flat_rows(k)] = jnp.broadcast_to(s, (cells, LANES))
            slope_keep[layer, flat_rows(k)] = slope
            return carry

        lax.fori_loop(0, height // ROWS, block, 0)

    def backward(layer, k, g, slot):
        flat = flat_rows(k)
        dh = backward_block(
            g,
            n_keep[layer, flat],
            s_keep[layer, flat][:, 0:1],
            slope_keep[layer, flat],
            gains[layer : layer + 1],
            w_in[layer],
            w_out[layer],
        )
        cotangent[slot, pl.ds(k * ROWS, ROWS)] = dh.reshape(ROWS, width, channels)

    prepare(0, x)

    count, obs_channels = obs_values.shape
    hits = owner[...] == lax.broadcasted_iota(jnp.int32, (count, LANES), 1)
    hits = hits.astype(f32)
    order = lax.broadcasted_iota(jnp.int32, (count, count), 1)
    place = lax.broadcasted_iota(jnp.int32, (count, count), 0)
    earlier = dot((order < place).astype(f32).astype(bf16), hits.astype(bf16))
    rank = jnp.sum(hits * earlier, axis=1, keepdims=True).astype(jnp.int32)
    slot = owner[...] * capacity + rank
    hot = (lax.broadcasted_iota(jnp.int32, (count, slots), 1) == slot).astype(f32).astype(bf16)
    lane = lax.broadcasted_iota(jnp.int32, (count, LANES), 1)
    parts = jnp.where(lane == 0, cell[...] // 64, jnp.where(lane == 1, cell[...] % 64, jnp.where(lane == 2, 1, 0)))
    content = jnp.concatenate([obs_values[...], parts.astype(f32).astype(bf16)], axis=1)
    outbox[...] = lax.dot_general(
        hot, content, (((0,), (0,)), ((), ())), preferred_element_type=f32
    ).astype(outbox.dtype)

    pl.semaphore_wait(barrier, grid)
    copies = launch(0, x)

    def box(k):
        to = lax.rem(me + k, grid)
        return pltpu.make_async_remote_copy(
            src_ref=outbox.at[pl.ds(pl.multiple_of(to * capacity, capacity), capacity)],
            dst_ref=inbox.at[pl.ds(pl.multiple_of(me * capacity, capacity), capacity)],
            send_sem=box_send.at[k],
            recv_sem=box_recv.at[k],
            device_id=peer(k),
            device_id_type=MESH,
        )

    def post(k, carry):
        box(k).start()
        return carry

    lax.fori_loop(1, grid, post, 0)
    own = pl.ds(pl.multiple_of(me * capacity, capacity), capacity)
    inbox[own] = outbox[own]

    receive(0, copies)
    forward(0, x, middle)
    copies = send(1, middle)
    receive(1, copies)
    forward(1, middle, last)

    def collect(k, carry):
        box(k).wait()
        return carry

    lax.fori_loop(1, grid, collect, 0)
    chunk = slots // 4
    state = last[...].reshape(height * width, channels)
    lane8 = lax.broadcasted_iota(jnp.int32, (LANES, LANES), 1)
    pick = jnp.where(lane8 == 0, 64.0, jnp.where(lane8 < 3, 1.0, 0.0)).astype(bf16)
    exchanges = []
    for k in range(4):
        at = slice(k * chunk, (k + 1) * chunk)
        where_from = dot_t(inbox[at, obs_channels:].astype(bf16), pick)[:, 0:1].astype(jnp.int32) - 1
        places = lax.broadcasted_iota(jnp.int32, (chunk, height * width), 1)
        chosen = (places == where_from).astype(f32).astype(bf16)
        picked = dot(chosen, state).astype(bf16)
        mine[at] = dot(picked, op[...]).astype(bf16)
        copy = pltpu.make_async_remote_copy(
            src_ref=mine.at[at],
            dst_ref=other.at[at],
            send_sem=ens_send.at[k],
            recv_sem=ens_recv.at[k],
            device_id=partner,
            device_id_type=MESH,
        )
        copy.start()
        exchanges.append(copy)
    cells_row = dot_t(pick[0:16], inbox[:, obs_channels:].astype(bf16))[0:1].astype(jnp.int32) - 1
    for copy in exchanges:
        copy.wait()
    mean_pred = (mine[...].astype(f32) + other[...].astype(f32)) * (1.0 / members)
    misfit = mean_pred - inbox[:, 0:obs_channels].astype(f32)
    adj = (precision[...] * misfit * (1.0 / members)).astype(bf16)

    def spread(k, carry):
        places = lax.broadcasted_iota(jnp.int32, (cells, slots), 0) + k * cells
        chosen = (places == cells_row).astype(f32).astype(bf16)
        total = dot(chosen, adj)
        high = total.astype(bf16)
        low = (total - high.astype(f32)).astype(bf16)
        g = dot_t(high, op[...]) + dot_t(low, op[...])
        grad[flat_rows(k)] = g
        backward(1, k, g, 0)
        return carry

    lax.fori_loop(0, height // ROWS, spread, 0)
    copies = send(2, cotangent.at[0])
    receive(2, copies)

    def inner(k, carry):
        conv_rows(xs, taps.at[1], hb, k * ROWS, True)
        g = grad[flat_rows(k)] + hb[...].reshape(cells, channels)
        grad[flat_rows(k)] = g
        backward(0, k, g, 1)
        return carry

    lax.fori_loop(0, height // ROWS, inner, 0)
    copies = send(3, cotangent.at[1])
    receive(3, copies)

    def outer(k, carry):
        rows = pl.ds(k * ROWS, ROWS)
        conv_rows(xs, taps.at[0], hb, k * ROWS, True)
        diff = x[rows].astype(f32) - background[rows].astype(f32)
        prior = prior_precision[...] * diff.reshape(cells, channels)
        total = prior + (grad[flat_rows(k)] + hb[...].reshape(cells, channels))
        out[rows] = total.reshape(ROWS, width, channels)
        return carry

    lax.fori_loop(0, height // ROWS, outer, 0)


def per_device(
    mesh_shape,
    initial_state,
    background,
    background_precision,
    kernel_taps,
    norm_gains,
    weight_in,
    weight_out,
    obs_operator,
    obs_precision,
    obs_values,
    obs_owner,
    obs_cell,
):
    f32, bf16 = jnp.float32, jnp.bfloat16
    height, width, channels = initial_state.shape[1:]
    hidden = weight_in.shape[2]
    cells = height * width
    obs_channels = obs_values.shape[1]
    grid = mesh_shape[0] * mesh_shape[1]
    capacity = 2 * obs_values.shape[0] // grid
    slots = grid * capacity
    box_type = bf16 if capacity % 16 == 0 else f32
    whole = pl.BlockSpec(memory_space=pltpu.VMEM)
    args = (
        initial_state[0],
        background[0],
        background_precision[None, :],
        kernel_taps,
        norm_gains,
        weight_in,
        weight_out,
        obs_operator,
        obs_precision[None, :],
        obs_values,
        obs_owner,
        obs_cell[:, None],
    )
    out = pl.pallas_call(
        functools.partial(kernel, mesh_shape),
        out_shape=jax.ShapeDtypeStruct((height, width, channels), f32),
        in_specs=[whole] * len(args),
        out_specs=whole,
        scratch_shapes=[
            pltpu.VMEM((height, width, channels), bf16),
            pltpu.VMEM((height, width, channels), bf16),
            pltpu.VMEM((2, height, width, channels), bf16),
            pltpu.VMEM((cells, channels), f32),
            pltpu.VMEM((2, cells, channels), bf16),
            pltpu.VMEM((2, cells, LANES), f32),
            pltpu.VMEM((2, cells, hidden), bf16),
            pltpu.VMEM((height + 4, width + 16, channels), f32),
            pltpu.VMEM((5, height + 4, width, channels), f32),
            pltpu.VMEM((ROWS, width, channels), f32),
            pltpu.VMEM((4, 2, 2 * height, channels), f32),
            pltpu.VMEM((4, 4, 8, channels), f32),
            pltpu.VMEM((4, 2, 2, width, channels), bf16),
            pltpu.VMEM((4, 2, 2 * height, channels), f32),
            pltpu.VMEM((4, 4, 8, channels), f32),
            pltpu.VMEM((slots, obs_channels + LANES), box_type),
            pltpu.VMEM((slots, obs_channels + LANES), box_type),
            pltpu.VMEM((slots, obs_channels), bf16),
            pltpu.VMEM((slots, obs_channels), bf16),
            pltpu.SemaphoreType.DMA((4, 8)),
            pltpu.SemaphoreType.DMA((4, 8)),
            pltpu.SemaphoreType.DMA((grid,)),
            pltpu.SemaphoreType.DMA((grid,)),
            pltpu.SemaphoreType.DMA((4,)),
            pltpu.SemaphoreType.DMA((4,)),
        ],
        compiler_params=pltpu.CompilerParams(
            vmem_limit_bytes=VMEM_BYTES, collective_id=0, has_side_effects=True
        ),
    )(*args)
    return out[None]


def solution(mesh):
    mesh_shape = (mesh.shape["lat"], mesh.shape["lon"], mesh.shape["ens"])
    in_specs = (
        P("ens", "lat", "lon", None),
        P("ens", "lat", "lon", None),
        P(),
        P(),
        P(),
        P(),
        P(),
        P(),
        P(),
        P(("lat", "lon"), None),
        P(("lat", "lon"), None),
        P(("lat", "lon")),
    )
    out_specs = P("ens", "lat", "lon", None)
    return jax.shard_map(
        functools.partial(per_device, mesh_shape), mesh=mesh, in_specs=in_specs, out_specs=out_specs, check_vma=False
    )
```

```python
import functools

import jax
import jax.numpy as jnp
from jax import lax
from jax.experimental import pallas as pl
from jax.experimental.pallas import tpu as pltpu
from jax.sharding import PartitionSpec as P

SQRT_TWO_OVER_PI = 0.7978845608
CUBIC = 0.044715
EPSILON = 1e-06
LANES = 128
ROWS = 8
VMEM_BYTES = 56 * 1024 * 1024


def dot(a, b):
    return jnp.dot(a, b, preferred_element_type=jnp.float32)


def dot_t(a, b):
    return lax.dot_general(a, b, (((1,), (1,)), ((), ())), preferred_element_type=jnp.float32)


DIRECTIONS = ((-1, 0), (1, 0), (0, -1), (0, 1), (-1, -1), (-1, 1), (1, -1), (1, 1))
MESH = pl.DeviceIdType.MESH


def conv_rows(xs, taps, out, r0, flip):
    width, channels = xs.shape[2], xs.shape[3]

    def column(step, carry):
        c0 = pl.multiple_of(step * 8, 8)
        for part in range(channels // LANES):
            lanes = slice(part * LANES, (part + 1) * LANES)
            acc = None
            for j in range(5):
                xj = xs[j, pl.ds(r0, ROWS + 4), pl.ds(c0, 8), lanes]
                for i in range(5):
                    at = 24 - (5 * i + j) if flip else 5 * i + j
                    term = taps[at : at + 1, lanes][None] * xj[i : i + ROWS]
                    acc = term if acc is None else acc + term
            out[:, pl.ds(c0, 8), lanes] = acc
        return carry

    lax.fori_loop(0, width // 8, column, 0, unroll=2)


def forward_block(h, x, gain, w_in, w_out):
    s = lax.rsqrt(jnp.mean(h * h, axis=1, keepdims=True) + EPSILON)
    n = (h * s * gain).astype(jnp.bfloat16)
    z = dot(n, w_in)
    zz = z * z
    inner = jnp.tanh(z * (SQRT_TWO_OVER_PI + (SQRT_TWO_OVER_PI * CUBIC) * zz))
    half = 0.5 + 0.5 * inner
    t = (z * half).astype(jnp.bfloat16)
    slope = half + (z * (0.5 - 0.5 * inner * inner)) * (
        SQRT_TWO_OVER_PI + (SQRT_TWO_OVER_PI * 3.0 * CUBIC) * zz
    )
    mixed = dot(t, w_out)
    return s, n, slope.astype(jnp.bfloat16), (x.astype(jnp.float32) + mixed).astype(jnp.bfloat16)


def backward_block(g, n, s, slope, gain, w_in, w_out):
    u = dot_t(g.astype(jnp.bfloat16), w_out)
    dz = (u * slope.astype(jnp.float32)).astype(jnp.bfloat16)
    dn = dot_t(dz, w_in)
    nf = n.astype(jnp.float32)
    m = jnp.mean(dn * nf, axis=1, keepdims=True)
    return (s * (gain * dn - (nf * (1.0 / gain)) * m)).astype(jnp.bfloat16)


def kernel(
    mesh_shape,
    x,
    background,
    prior_precision,
    tap_rows,
    gains,
    w_in,
    w_out,
    op,
    precision,
    obs_values,
    owner,
    cell,
    out,
    middle,
    last,
    cotangent,
    grad,
    n_keep,
    s_keep,
    slope_keep,
    xp,
    xs,
    hb,
    stage_side,
    stage_corner,
    got_edge,
    got_side,
    got_corner,
    outbox,
    inbox,
    mine,
    other,
    halo_send,
    halo_recv,
    box_send,
    box_recv,
    ens_send,
    ens_recv,
    taps,
):
    f32, bf16 = jnp.float32, jnp.bfloat16
    lats, lons, members = mesh_shape
    height, width, channels = x.shape
    lat, lon, ens = lax.axis_index("lat"), lax.axis_index("lon"), lax.axis_index("ens")
    grid = lats * lons
    me = lat * lons + lon
    slots = inbox.shape[0]
    capacity = slots // grid
    partner = {"lat": lat, "lon": lon, "ens": 1 - ens}
    cells = ROWS * width

    def peer(k):
        to = lax.rem(me + k, grid)
        return {"lat": to // lons, "lon": lax.rem(to, lons), "ens": ens}

    barrier = pltpu.get_barrier_semaphore()

    def greet(k, carry):
        pl.semaphore_signal(barrier, inc=1, device_id=peer(k), device_id_type=MESH)
        return carry

    lax.fori_loop(1, grid, greet, 0)
    pl.semaphore_signal(barrier, inc=1, device_id=partner, device_id_type=MESH)

    def prepare(step, field):
        def fill(k, carry):
            r = k * 4
            xp[pl.ds(r + 2, 4), 8 : 8 + width] = field[pl.ds(r, 4)].astype(f32)
            return carry

        lax.fori_loop(0, height // 4, fill, 0)
        for side, first in ((0, 8), (1, 6 + width)):
            for c in range(2):
                stage_side[step, side, c * height : (c + 1) * height] = xp[2 : 2 + height, first + c, :]
        for k, (down, east) in enumerate(DIRECTIONS[4:]):
            r0 = 2 if down < 0 else height
            c0 = 8 if east < 0 else 6 + width
            for r in range(2):
                stage_corner[step, k, 4 * r : 4 * r + 2] = xp[r0 + r, c0 : c0 + 2, :]

    def launch(step, field):
        copies = []
        for d, (down, east) in enumerate(DIRECTIONS):
            if d < 2:
                source = field.at[0:2] if down < 0 else field.at[height - 2 : height]
                target = got_edge.at[step, d]
            elif d < 4:
                source, target = stage_side.at[step, d - 2], got_side.at[step, d - 2]
            else:
                source, target = stage_corner.at[step, d - 4], got_corner.at[step, d - 4]
            copy = pltpu.make_async_remote_copy(
                src_ref=source,
                dst_ref=target,
                send_sem=halo_send.at[step, d],
                recv_sem=halo_recv.at[step, d],
                device_id={
                    "lat": lax.rem(lat + down + lats, lats),
                    "lon": lax.rem(lon + east + lons, lons),
                    "ens": ens,
                },
                device_id_type=MESH,
            )
            copy.start()
            copies.append(copy)

        def shift(k, carry):
            r = k * 4 + 2
            for j in range(5):
                xs[j, pl.ds(r, 4)] = xp[pl.ds(r, 4), 6 + j : 6 + j + width]
            return carry

        lax.fori_loop(0, height // 4, shift, 0)
        return copies

    def send(step, field):
        prepare(step, field)
        return launch(step, field)

    def receive(step, copies):
        for copy in copies:
            copy.wait()
        above = (lat > 0).astype(f32)
        below = (lat < lats - 1).astype(f32)
        xp[height + 2 : height + 4, 8 : 8 + width] = got_edge[step, 0].astype(f32) * below
        xp[0:2, 8 : 8 + width] = got_edge[step, 1].astype(f32) * above
        for side, first in ((0, 8 + width), (1, 6)):
            for c in range(2):
                xp[2 : 2 + height, first + c, :] = got_side[step, side, c * height : (c + 1) * height]
        for k, (down, east) in enumerate(DIRECTIONS[4:]):
            r0, keep = (height + 2, below) if down < 0 else (0, above)
            c0 = 8 + width if east < 0 else 6
            for r in range(2):
                xp[r0 + r, c0 : c0 + 2, :] = got_corner[step, k, 4 * r : 4 * r + 2] * keep

        for r in (0, height + 2):
            for j in range(5):
                xs[j, r : r + 2] = xp[r : r + 2, 6 + j : 6 + j + width]

        def shift(k, carry):
            rows = pl.ds(k * 8 + 2, 8)
            for j in (0, 1):
                xs[j, rows, 0:8] = xp[rows, 6 + j : 14 + j]
            for j in (3, 4):
                xs[j, rows, width - 8 : width] = xp[rows, width - 2 + j : width + 6 + j]
            return carry

        lax.fori_loop(0, height // 8, shift, 0)

    def flat_rows(k):
        return pl.ds(pl.multiple_of(k * cells, cells), cells)

    def forward(layer, field, new_field):
        def block(k, carry):
            rows = pl.ds(k * ROWS, ROWS)
            conv_rows(xs, taps.at[layer], hb, k * ROWS, False)
            s, n, slope, new = forward_block(
                hb[...].reshape(cells, channels),
                field[rows].reshape(cells, channels),
                gains[layer : layer + 1],
                w_in[layer],
                w_out[layer],
            )
            new_field[rows] = new.reshape(ROWS, width, channels)
            n_keep[layer, flat_rows(k)] = n
            s_keep[layer, flat_rows(k)] = jnp.broadcast_to(s, (cells, LANES))
            slope_keep[layer, flat_rows(k)] = slope
            return carry

        lax.fori_loop(0, height // ROWS, block, 0)

    def backward(layer, k, g, slot):
        flat = flat_rows(k)
        dh = backward_block(
            g,
            n_keep[layer, flat],
            s_keep[layer, flat][:, 0:1],
            slope_keep[layer, flat],
            gains[layer : layer + 1],
            w_in[layer],
            w_out[layer],
        )
        cotangent[slot, pl.ds(k * ROWS, ROWS)] = dh.reshape(ROWS, width, channels)

    prepare(0, x)
    for t in range(tap_rows.shape[0]):
        for layer in range(2):
            taps[layer, t : t + 1] = tap_rows[t, layer : layer + 1]

    count, obs_channels = obs_values.shape
    hits = (owner[...] == lax.broadcasted_iota(jnp.int32, (LANES, count), 0)).astype(f32)
    order = lax.broadcasted_iota(jnp.int32, (count, count), 0)
    place = lax.broadcasted_iota(jnp.int32, (count, count), 1)
    earlier = dot(hits.astype(bf16), (order < place).astype(f32).astype(bf16))
    rank = jnp.sum(hits * earlier, axis=0, keepdims=True).astype(jnp.int32)
    slot = owner[...] * capacity + rank
    hot = (lax.broadcasted_iota(jnp.int32, (slots, count), 0) == slot).astype(f32).astype(bf16)
    line = lax.broadcasted_iota(jnp.int32, (LANES, count), 0)
    parts = jnp.where(line == 0, cell[...] // 64, jnp.where(line == 1, cell[...] % 64, jnp.where(line == 2, 1, 0)))
    outbox[:, 0:obs_channels] = dot(hot, obs_values[...]).astype(outbox.dtype)
    outbox[:, obs_channels:] = dot_t(hot, parts.astype(f32).astype(bf16)).astype(outbox.dtype)

    pl.semaphore_wait(barrier, grid)
    copies = launch(0, x)

    def box(k):
        to = lax.rem(me + k, grid)
        return pltpu.make_async_remote_copy(
            src_ref=outbox.at[pl.ds(pl.multiple_of(to * capacity, capacity), capacity)],
            dst_ref=inbox.at[pl.ds(pl.multiple_of(me * capacity, capacity), capacity)],
            send_sem=box_send.at[k],
            recv_sem=box_recv.at[k],
            device_id=peer(k),
            device_id_type=MESH,
        )

    def post(k, carry):
        box(k).start()
        return carry

    lax.fori_loop(1, grid, post, 0)
    own = pl.ds(pl.multiple_of(me * capacity, capacity), capacity)
    inbox[own] = outbox[own]

    receive(0, copies)
    forward(0, x, middle)
    copies = send(1, middle)
    receive(1, copies)
    forward(1, middle, last)

    def collect(k, carry):
        box(k).wait()
        return carry

    lax.fori_loop(1, grid, collect, 0)
    chunk = slots // 4
    state = last[...].reshape(height * width, channels)
    lane8 = lax.broadcasted_iota(jnp.int32, (LANES, LANES), 1)
    pick = jnp.where(lane8 == 0, 64.0, jnp.where(lane8 < 3, 1.0, 0.0)).astype(bf16)
    exchanges = []
    for k in range(4):
        at = slice(k * chunk, (k + 1) * chunk)
        where_from = dot_t(inbox[at, obs_channels:].astype(bf16), pick)[:, 0:1].astype(jnp.int32) - 1
        places = lax.broadcasted_iota(jnp.int32, (chunk, height * width), 1)
        chosen = (places == where_from).astype(f32).astype(bf16)
        picked = dot(chosen, state).astype(bf16)
        mine[at] = dot(picked, op[...]).astype(bf16)
        copy = pltpu.make_async_remote_copy(
            src_ref=mine.at[at],
            dst_ref=other.at[at],
            send_sem=ens_send.at[k],
            recv_sem=ens_recv.at[k],
            device_id=partner,
            device_id_type=MESH,
        )
        copy.start()
        exchanges.append(copy)
    cells_row = dot_t(pick[0:16], inbox[:, obs_channels:].astype(bf16))[0:1].astype(jnp.int32) - 1
    for copy in exchanges:
        copy.wait()
    mean_pred = (mine[...].astype(f32) + other[...].astype(f32)) * (1.0 / members)
    misfit = mean_pred - inbox[:, 0:obs_channels].astype(f32)
    adj = (precision[...] * misfit * (1.0 / members)).astype(bf16)

    def spread(k, carry):
        places = lax.broadcasted_iota(jnp.int32, (cells, slots), 0) + k * cells
        chosen = (places == cells_row).astype(f32).astype(bf16)
        total = dot(chosen, adj)
        high = total.astype(bf16)
        low = (total - high.astype(f32)).astype(bf16)
        g = dot_t(high, op[...]) + dot_t(low, op[...])
        grad[flat_rows(k)] = g
        backward(1, k, g, 0)
        return carry

    lax.fori_loop(0, height // ROWS, spread, 0)
    copies = send(2, cotangent.at[0])
    receive(2, copies)

    def inner(k, carry):
        conv_rows(xs, taps.at[1], hb, k * ROWS, True)
        g = grad[flat_rows(k)] + hb[...].reshape(cells, channels)
        grad[flat_rows(k)] = g
        backward(0, k, g, 1)
        return carry

    lax.fori_loop(0, height // ROWS, inner, 0)
    copies = send(3, cotangent.at[1])
    receive(3, copies)

    def outer(k, carry):
        rows = pl.ds(k * ROWS, ROWS)
        conv_rows(xs, taps.at[0], hb, k * ROWS, True)
        diff = x[rows].astype(f32) - background[rows].astype(f32)
        prior = prior_precision[...] * diff.reshape(cells, channels)
        total = prior + (grad[flat_rows(k)] + hb[...].reshape(cells, channels))
        out[rows] = total.reshape(ROWS, width, channels)
        return carry

    lax.fori_loop(0, height // ROWS, outer, 0)


def per_device(
    mesh_shape,
    initial_state,
    background,
    background_precision,
    kernel_taps,
    norm_gains,
    weight_in,
    weight_out,
    obs_operator,
    obs_precision,
    obs_values,
    obs_owner,
    obs_cell,
):
    f32, bf16 = jnp.float32, jnp.bfloat16
    height, width, channels = initial_state.shape[1:]
    hidden = weight_in.shape[2]
    cells = height * width
    obs_channels = obs_values.shape[1]
    grid = mesh_shape[0] * mesh_shape[1]
    capacity = 2 * obs_values.shape[0] // grid
    slots = grid * capacity
    box_type = bf16 if capacity % 16 == 0 else f32
    whole = pl.BlockSpec(memory_space=pltpu.VMEM)
    args = (
        initial_state[0],
        background[0],
        background_precision[None, :],
        jnp.swapaxes(kernel_taps, 0, 1),
        norm_gains,
        weight_in,
        weight_out,
        obs_operator,
        obs_precision[None, :],
        obs_values,
        obs_owner.reshape(1, -1),
        obs_cell[None, :],
    )
    out = pl.pallas_call(
        functools.partial(kernel, mesh_shape),
        out_shape=jax.ShapeDtypeStruct((height, width, channels), f32),
        in_specs=[whole] * len(args),
        out_specs=whole,
        scratch_shapes=[
            pltpu.VMEM((height, width, channels), bf16),
            pltpu.VMEM((height, width, channels), bf16),
            pltpu.VMEM((2, height, width, channels), bf16),
            pltpu.VMEM((cells, channels), f32),
            pltpu.VMEM((2, cells, channels), bf16),
            pltpu.VMEM((2, cells, LANES), f32),
            pltpu.VMEM((2, cells, hidden), bf16),
            pltpu.VMEM((height + 4, width + 16, channels), f32),
            pltpu.VMEM((5, height + 4, width, channels), f32),
            pltpu.VMEM((ROWS, width, channels), f32),
            pltpu.VMEM((4, 2, 2 * height, channels), f32),
            pltpu.VMEM((4, 4, 8, channels), f32),
            pltpu.VMEM((4, 2, 2, width, channels), bf16),
            pltpu.VMEM((4, 2, 2 * height, channels), f32),
            pltpu.VMEM((4, 4, 8, channels), f32),
            pltpu.VMEM((slots, obs_channels + LANES), box_type),
            pltpu.VMEM((slots, obs_channels + LANES), box_type),
            pltpu.VMEM((slots, obs_channels), bf16),
            pltpu.VMEM((slots, obs_channels), bf16),
            pltpu.SemaphoreType.DMA((4, 8)),
            pltpu.SemaphoreType.DMA((4, 8)),
            pltpu.SemaphoreType.DMA((grid,)),
            pltpu.SemaphoreType.DMA((grid,)),
            pltpu.SemaphoreType.DMA((4,)),
            pltpu.SemaphoreType.DMA((4,)),
            pltpu.VMEM(kernel_taps.shape, f32),
        ],
        compiler_params=pltpu.CompilerParams(
            vmem_limit_bytes=VMEM_BYTES, collective_id=0, has_side_effects=True
        ),
    )(*args)
    return out[None]


def solution(mesh):
    mesh_shape = (mesh.shape["lat"], mesh.shape["lon"], mesh.shape["ens"])
    in_specs = (
        P("ens", "lat", "lon", None),
        P("ens", "lat", "lon", None),
        P(),
        P(),
        P(),
        P(),
        P(),
        P(),
        P(),
        P(("lat", "lon"), None),
        P(("lat", "lon"), None),
        P(("lat", "lon")),
    )
    out_specs = P("ens", "lat", "lon", None)
    return jax.shard_map(
        functools.partial(per_device, mesh_shape), mesh=mesh, in_specs=in_specs, out_specs=out_specs, check_vma=False
    )
```
